32 devices in a mesh: grp: 2 (over x), feat: 8 (over z, y), tok: 2 (over core).
Axes of the slice: x: 2, y: 2, z: 4, core: 2. Of those that a mesh axis runs over, the one named last changes fastest.
Arguments:
- tokens: bfloat16 [2048, 8192], P(('grp', 'tok'), 'feat'), parts along dimension 0, may hold values from -6 to 6
- in_weight: bfloat16 [8192, 3, 8192], P('tok', None, 'feat'), may hold values from -0.0625 to 0.0625
- filters: float32 [512, 128], P('feat'), may hold values from -0.5 to 0.5
- out_weight: bfloat16 [8192, 8192], P('feat'), may hold values from -0.09375 to 0.09375
Outputs:
- mixed_out: bfloat16 [2048, 8192], P(('grp', 'tok'), 'feat'), parts along dimension 0
The draws below stay inside these ranges and needn't reach their ends.
There are 2 independent parts, one for each index of `grp`. The reference program is written for one: setup_inputs(seed, part) draws one part's arguments, and reference() takes and returns one part's arrays. A program takes and returns all parts, laid end to end along the dimension named above; an argument that names none is the same for every part. Nothing has to cross between parts.
All inputs are finite; a program needn't handle non-finite values.
Results may differ from the reference program's by a relative error of at most 0.024.
Values may be sent and summed in bfloat16 or wider, within the bound.
A program may use at most 192 MiB of HBM per device.

```python
import jax
import jax.numpy as jnp
from jax import lax

D = 8192
KLEN = 128
GROUP = 16
TOKENS = 1024
FILTERS = 512


def with_spikes(array, own_key, source, target, parts, factor):
    def block_of(position):
        return (jnp.arange(array.shape[position]) // (array.shape[position] // parts)).reshape((-1,) + (1,) * (array.ndim - 1 - position))

    first = jax.random.permutation(own_key, parts)[block_of(target)]
    far = (block_of(target) + parts // 2) % parts
    return jnp.where((block_of(source) == first) | (block_of(source) == far), factor * array, array)


def block_scale(rng, dims, cuts, low, top_value):
    factor_of = 1.0
    for position, shards_of in cuts:
        draws = jax.random.uniform(jax.random.fold_in(jax.random.fold_in(rng, 6), position), (shards_of,), jnp.float32, low / len(cuts), top_value / len(cuts))
        factor_of = factor_of * jnp.repeat(jnp.exp(draws), dims[position] // shards_of).reshape((-1,) + (1,) * (len(dims) - 1 - position))
    return factor_of


def normal_values(own_key, dims, scale, limit, cuts=(), held_as=jnp.bfloat16):
    entries = jax.random.normal(own_key, dims, jnp.float32) * scale
    if len(cuts) > 0:
        entries = block_scale(own_key, dims, cuts, -0.22, 0.18) * entries
    return jnp.clip(entries, min=-limit, max=limit).astype(held_as)


def heavy_noise(stream_key, shape, deviation, reach, shards, heavy, kind=jnp.bfloat16):
    result = deviation * jax.random.normal(stream_key, shape, jnp.float32)
    if shards:
        result = result * block_scale(stream_key, shape, shards, -0.22, 0.18)
    return jnp.clip(with_spikes(result, jax.random.fold_in(stream_key, 3), *heavy), -reach, reach).astype(kind)


def setup_inputs(seed: int = 0, part: int = 0) -> dict:
    streams_of = jax.random.split(jax.random.key(seed), 5)
    part_keys = jax.random.split(jax.random.fold_in(streams_of[4], part), 5)
    return {
        "tokens": normal_values(part_keys[0], (TOKENS, D), 1.0, 6.0, ((0, 2), (1, 8))),
        "in_weight": normal_values(streams_of[1], (D, 3, D), D ** -0.5, 0.0625, ((0, 2), (2, 8))),
        "filters": normal_values(streams_of[2], (FILTERS, KLEN), 0.09, 0.5, ((0, 8),), jnp.float32),
        "out_weight": heavy_noise(streams_of[3], (D, D), D ** -0.5, 0.09375, ((0, 8),), (0, 1, 8, 2.0)),
    }


def reference(tokens, in_weight, filters, out_weight):
    count = tokens.shape[0]
    width = tokens.shape[1]
    proj = jnp.dot(tokens, in_weight.reshape(width, 3 * width), preferred_element_type=jnp.float32).astype(jnp.bfloat16)
    proj = proj.reshape(count, 3, width)
    query = proj[:, 0, :].astype(jnp.float32)
    gated = (proj[:, 1, :].astype(jnp.float32) * proj[:, 2, :].astype(jnp.float32)).astype(jnp.bfloat16)
    halo = KLEN - 1
    extended = jnp.concatenate([jnp.zeros((halo, width), jnp.float32), gated.astype(jnp.float32)], axis=0)
    taps = jnp.repeat(filters, GROUP, axis=0).T

    def add_tap(j, total):
        window = lax.dynamic_slice_in_dim(extended, (halo - j).astype(jnp.int32), count, 0)
        coeff = lax.dynamic_index_in_dim(taps, j.astype(jnp.int32), 0, keepdims=True)
        return total + window * coeff

    conv = lax.fori_loop(0, KLEN, add_tap, jnp.zeros((count, width), jnp.float32))
    hidden = (query * conv).astype(jnp.bfloat16)
    return jnp.dot(hidden, out_weight, preferred_element_type=jnp.float32).astype(jnp.bfloat16)
```

```python
import functools

import jax
import jax.numpy as jnp
from jax import lax
from jax.experimental import pallas as pl
from jax.experimental.pallas import tpu as pltpu
from jax.sharding import PartitionSpec as P

GROUP = 16
LANES = 128


def conv_kernel(band_ref, q_ref, k_ref, v_ref, out_ref):
    taps = band_ref.shape[2] // 2
    rows = q_ref.shape[0]
    blocks = rows // taps
    gated = (k_ref[...].astype(jnp.float32) * v_ref[...].astype(jnp.float32)).astype(jnp.bfloat16)
    right = jnp.concatenate(
        [gated[b * taps : (b + 2) * taps] for b in range(blocks)], axis=1
    )
    lane = lax.broadcasted_iota(jnp.int32, (taps, LANES), 1) // GROUP
    lane = jnp.concatenate([lane] * blocks, axis=1)
    total = jnp.zeros((taps, blocks * LANES), jnp.float32)
    for f in range(LANES // GROUP):
        row = jnp.broadcast_to(band_ref[0, f : f + 1, :], (taps, 2 * taps))
        band = pltpu.roll(row, 0, 1, stride=1, stride_axis=0).astype(jnp.bfloat16)
        product = jnp.dot(band, right, preferred_element_type=jnp.float32)
        total = jnp.where(lane == f, product, total)
    for b in range(blocks):
        at = slice(b * taps, (b + 1) * taps)
        out_ref[at, :] = (
            q_ref[at, :].astype(jnp.float32) * total[:, b * LANES : (b + 1) * LANES]
        ).astype(jnp.bfloat16)


def convolve(filters, query, keyed, valued):
    rows, channels = query.shape
    count, taps = filters.shape
    per = LANES // GROUP
    band = jnp.concatenate(
        [jnp.zeros((count, 1), jnp.float32), filters[:, ::-1], jnp.zeros((count, taps - 1), jnp.float32)],
        axis=1,
    ).reshape(count // per, per, 2 * taps)
    return pl.pallas_call(
        conv_kernel,
        grid=(channels // LANES,),
        out_shape=jax.ShapeDtypeStruct((rows, channels), jnp.bfloat16),
        in_specs=[
            pl.BlockSpec((1, per, 2 * taps), lambda i: (i, 0, 0)),
            pl.BlockSpec((rows, LANES), lambda i: (0, i)),
            pl.BlockSpec((rows + taps, LANES), lambda i: (0, i)),
            pl.BlockSpec((rows + taps, LANES), lambda i: (0, i)),
        ],
        out_specs=pl.BlockSpec((rows, LANES), lambda i: (0, i)),
        compiler_params=pltpu.CompilerParams(vmem_limit_bytes=24 * 1024 * 1024),
    )(band, query, keyed, valued)


def swap(block):
    return lax.ppermute(block, "tok", [(0, 1), (1, 0)])


def shards(tokens, in_weight, filters, out_weight):
    rows = tokens.shape[0]
    depth = in_weight.shape[0]
    channels = in_weight.shape[2]
    taps = filters.shape[1]
    me = lax.axis_index("tok")
    panel = jnp.transpose(in_weight, (1, 0, 2))
    full = lax.all_gather(tokens, "feat", axis=1, tiled=True)
    mine = lax.dynamic_slice_in_dim(full, me * depth, depth, 1)
    theirs = swap(lax.dynamic_slice_in_dim(full, (1 - me) * depth, depth, 1))

    def project(x):
        return [jnp.dot(x, panel[s], preferred_element_type=jnp.float32) for s in range(3)]

    away = [swap(p.astype(jnp.bfloat16)) for p in project(theirs)]
    home = project(mine)
    q, k, v = [(a.astype(jnp.float32) + b).astype(jnp.bfloat16) for a, b in zip(away, home)]

    def extend(x):
        return jnp.concatenate([lax.ppermute(x[rows - taps :], "tok", [(0, 1)]), x], axis=0)

    hidden = convolve(filters, q, extend(k), extend(v))
    partial_rows = jnp.dot(hidden, out_weight, preferred_element_type=jnp.float32)
    return lax.psum_scatter(
        partial_rows.astype(jnp.bfloat16), "feat", scatter_dimension=1, tiled=True
    )


def solution(mesh):
    in_specs = (P(("grp", "tok"), "feat"), P("tok", None, "feat"), P("feat", None), P("feat", None))
    out_specs = P(("grp", "tok"), "feat")
    return jax.shard_map(shards, mesh=mesh, in_specs=in_specs, out_specs=out_specs, check_vma=False)
```

```python
import functools

import jax
import jax.numpy as jnp
from jax import lax
from jax.experimental import pallas as pl
from jax.experimental.pallas import tpu as pltpu
from jax.sharding import PartitionSpec as P

GROUP = 16
LANES = 128


def conv_kernel(band_ref, q_ref, k_ref, v_ref, out_ref):
    taps = band_ref.shape[2] // 2
    rows = q_ref.shape[0]
    blocks = rows // taps
    gated = (k_ref[...].astype(jnp.float32) * v_ref[...].astype(jnp.float32)).astype(jnp.bfloat16)
    right = jnp.concatenate(
        [gated[b * taps : (b + 2) * taps] for b in range(blocks)], axis=1
    )
    lane = lax.broadcasted_iota(jnp.int32, (taps, LANES), 1) // GROUP
    lane = jnp.concatenate([lane] * blocks, axis=1)
    total = jnp.zeros((taps, blocks * LANES), jnp.float32)
    for f in range(LANES // GROUP):
        row = jnp.broadcast_to(band_ref[0, f : f + 1, :], (taps, 2 * taps))
        band = pltpu.roll(row, 0, 1, stride=1, stride_axis=0).astype(jnp.bfloat16)
        product = jnp.dot(band, right, preferred_element_type=jnp.float32)
        total = jnp.where(lane == f, product, total)
    for b in range(blocks):
        at = slice(b * taps, (b + 1) * taps)
        out_ref[at, :] = (
            q_ref[at, :].astype(jnp.float32) * total[:, b * LANES : (b + 1) * LANES]
        ).astype(jnp.bfloat16)


def convolve(filters, query, keyed, valued):
    rows, channels = query.shape
    count, taps = filters.shape
    per = LANES // GROUP
    band = jnp.concatenate(
        [jnp.zeros((count, 1), jnp.float32), filters[:, ::-1], jnp.zeros((count, taps - 1), jnp.float32)],
        axis=1,
    ).reshape(count // per, per, 2 * taps)
    return pl.pallas_call(
        conv_kernel,
        grid=(channels // LANES,),
        out_shape=jax.ShapeDtypeStruct((rows, channels), jnp.bfloat16),
        in_specs=[
            pl.BlockSpec((1, per, 2 * taps), lambda i: (i, 0, 0)),
            pl.BlockSpec((rows, LANES), lambda i: (0, i)),
            pl.BlockSpec((rows + taps, LANES), lambda i: (0, i)),
            pl.BlockSpec((rows + taps, LANES), lambda i: (0, i)),
        ],
        out_specs=pl.BlockSpec((rows, LANES), lambda i: (0, i)),
        compiler_params=pltpu.CompilerParams(vmem_limit_bytes=24 * 1024 * 1024),
    )(band, query, keyed, valued)


def swap(block):
    return lax.ppermute(block, "tok", [(0, 1), (1, 0)])


def shards(tokens, in_weight, filters, out_weight):
    rows = tokens.shape[0]
    depth = in_weight.shape[0]
    channels = in_weight.shape[2]
    taps = filters.shape[1]
    me = lax.axis_index("tok")
    panel = jnp.transpose(in_weight, (1, 0, 2))
    cuts = 2
    step = rows // cuts

    def project(x):
        return [jnp.dot(x, panel[s], preferred_element_type=jnp.float32) for s in range(3)]

    pieces = []
    for c in range(cuts):
        block = tokens[c * step : (c + 1) * step]
        if c > 0:
            block, full = lax.optimization_barrier((block, full))
        full = lax.all_gather(block, "feat", axis=1, tiled=True)
        theirs = swap(lax.dynamic_slice_in_dim(full, (1 - me) * depth, depth, 1))
        home = project(lax.dynamic_slice_in_dim(full, me * depth, depth, 1))
        away = [swap(p.astype(jnp.bfloat16)) for p in project(theirs)]
        pieces.append([(a.astype(jnp.float32) + b).astype(jnp.bfloat16) for a, b in zip(away, home)])
    q, k, v = [jnp.concatenate(x, axis=0) for x in zip(*pieces)]

    def extend(x):
        return jnp.concatenate([lax.ppermute(x[rows - taps :], "tok", [(0, 1)]), x], axis=0)

    hidden = convolve(filters, q, extend(k), extend(v))
    results = []
    for c in range(cuts):
        partial_rows = jnp.dot(
            hidden[c * step : (c + 1) * step], out_weight, preferred_element_type=jnp.float32
        )
        results.append(
            lax.psum_scatter(
                partial_rows.astype(jnp.bfloat16), "feat", scatter_dimension=1, tiled=True
            )
        )
    return jnp.concatenate(results, axis=0)


def solution(mesh):
    in_specs = (P(("grp", "tok"), "feat"), P("tok", None, "feat"), P("feat", None), P("feat", None))
    out_specs = P(("grp", "tok"), "feat")
    return jax.shard_map(shards, mesh=mesh, in_specs=in_specs, out_specs=out_specs, check_vma=False)
```
